128 devices in a mesh: row: 8 (over y_hi, x), col: 16 (over y_lo, z, core).
Axes of the slice: x: 4, y: 4 (y_hi: 2, y_lo: 2; y = y_hi * 2 + y_lo), z: 4, core: 2. Of those that a mesh axis runs over, the one named last changes fastest.
Arguments:
- alignment_embedding: bfloat16 [256, 640, 256], P(('row', 'col')), may hold values from -6 to 6
- standardizer_scaling: float32 [256], replicated, may hold values from 0.1 to 1.9
- first_linear_map: bfloat16 [256, 32], replicated, may hold values from -0.375 to 0.375
- first_offset_terms: float32 [32], replicated, may hold values from -0.6 to 0.6
- second_linear_map: bfloat16 [256, 32], replicated, may hold values from -0.375 to 0.375
- second_offset_terms: float32 [32], replicated, may hold values from -0.6 to 0.6
- final_linear_map: bfloat16 [1024, 128], replicated, may hold values from -4 to 4
- final_offset_terms: float32 [128], replicated, may hold values from -3 to 3
- couple_embedding: bfloat16 [640, 640, 128], P('row', 'col'), may hold values from -6 to 6
Outputs:
- pair_out: bfloat16 [640, 640, 128], P('row', 'col')
The draws below stay inside these ranges and needn't reach their ends.
All inputs are finite; a program needn't handle non-finite values.
Results may differ from the reference program's by a relative error of at most 0.0067.
Values may be sent and summed in bfloat16 or wider, within the bound.
A program may use at most 128 MiB of HBM per device.

```python
import math
import jax
import jax.numpy as jnp
from jax import lax

ALIGN_FEATURES = 256
HIDDEN_FEATURES = 32
CP = 128
ALIGN_HOMOLOGS = 256
WINDOW_AMINOS = 640


def level_of(key, dims, split, least, high):
    level, own = 1.0, jax.random.fold_in(key, 6)
    for axis_at, parts in split:
        draws = jnp.exp(jax.random.uniform(jax.random.fold_in(own, axis_at), (parts,), jnp.float32, least / len(split), high / len(split)))
        level = level * jnp.repeat(draws, dims[axis_at] // parts).reshape([-1 if axis == axis_at else 1 for axis in range(len(dims))])
    return level


def centred(key, dims, scale, reach, split=(), kind=jnp.bfloat16):
    entries = jax.random.normal(key, dims, jnp.float32) * scale
    if len(split) > 0:
        entries = level_of(key, dims, split, -0.22, 0.18) * entries
    return jnp.clip(entries, min=-reach, max=reach).astype(kind)


def setup_inputs(seed: int = 0) -> dict:
    streams_of = jax.random.split(jax.random.key(seed), 10)
    alignment_embedding = centred(streams_of[0], (ALIGN_HOMOLOGS, WINDOW_AMINOS, ALIGN_FEATURES), 1.0, 6.0, ((0, 128),))
    standardizer_scaling = jnp.clip(1.0 + 0.18 * jax.random.normal(streams_of[1], (ALIGN_FEATURES,), jnp.float32), 0.1, 1.9)
    first_linear_map = centred(streams_of[2], (ALIGN_FEATURES, HIDDEN_FEATURES), ALIGN_FEATURES ** -0.5, 0.375)
    first_offset_terms = centred(streams_of[3], (HIDDEN_FEATURES,), 0.1, 0.6, (), jnp.float32)
    second_linear_map = centred(streams_of[4], (ALIGN_FEATURES, HIDDEN_FEATURES), ALIGN_FEATURES ** -0.5, 0.375)
    second_offset_terms = centred(streams_of[5], (HIDDEN_FEATURES,), 0.1, 0.6, (), jnp.float32)
    final_linear_map = centred(streams_of[6], (HIDDEN_FEATURES * HIDDEN_FEATURES, CP), 0.7, 4.0)
    final_offset_terms = centred(streams_of[7], (CP,), 0.5, 3.0, (), jnp.float32)
    couple_embedding = centred(streams_of[8], (WINDOW_AMINOS, WINDOW_AMINOS, CP), 1.0, 6.0, ((0, 8), (1, 16)))
    return {"alignment_embedding": alignment_embedding, "standardizer_scaling": standardizer_scaling, "first_linear_map": first_linear_map, "first_offset_terms": first_offset_terms, "second_linear_map": second_linear_map, "second_offset_terms": second_offset_terms, "final_linear_map": final_linear_map, "final_offset_terms": final_offset_terms, "couple_embedding": couple_embedding}


def reference(alignment_embedding, standardizer_scaling, first_linear_map, first_offset_terms, second_linear_map, second_offset_terms, final_linear_map, final_offset_terms, couple_embedding):
    averaged_tensor_entries = alignment_embedding.astype(jnp.float32)
    deviation_from_average = lax.optimization_barrier(jnp.mean(averaged_tensor_entries, axis=-1, keepdims=True))
    variability_estimate = lax.optimization_barrier(jnp.mean((averaged_tensor_entries - deviation_from_average) ** 2, axis=-1, keepdims=True))
    standardized_alignment = ((averaged_tensor_entries - deviation_from_average) / jnp.sqrt(variability_estimate + 1e-05) * standardizer_scaling).astype(jnp.bfloat16)
    unrolled_tensor_entries = standardized_alignment.reshape(ALIGN_HOMOLOGS * WINDOW_AMINOS, ALIGN_FEATURES)
    first_factor = (jnp.dot(unrolled_tensor_entries, first_linear_map, preferred_element_type=jnp.float32) + first_offset_terms).astype(jnp.bfloat16).reshape(ALIGN_HOMOLOGS, WINDOW_AMINOS, HIDDEN_FEATURES)
    second_factor = (jnp.dot(unrolled_tensor_entries, second_linear_map, preferred_element_type=jnp.float32) + second_offset_terms).astype(jnp.bfloat16).reshape(ALIGN_HOMOLOGS, WINDOW_AMINOS, HIDDEN_FEATURES)
    tile_portion = math.gcd(WINDOW_AMINOS, 32)
    right_wide = second_factor.astype(jnp.float32)

    def one_block(index):
        piece = lax.dynamic_slice_in_dim(first_factor, index * tile_portion, tile_portion, 1).astype(jnp.float32)
        accumulated_entries = jnp.einsum('sic,sje->ijce', piece, right_wide)
        tensor_entries = (accumulated_entries / ALIGN_HOMOLOGS).astype(jnp.bfloat16).reshape(tile_portion * WINDOW_AMINOS, HIDDEN_FEATURES * HIDDEN_FEATURES)
        update = jnp.dot(tensor_entries, final_linear_map, preferred_element_type=jnp.float32) + final_offset_terms
        rows = lax.dynamic_slice_in_dim(couple_embedding, index * tile_portion, tile_portion, 0).astype(jnp.float32)
        return (rows + update.reshape(tile_portion, WINDOW_AMINOS, CP)).astype(jnp.bfloat16)
    result = lax.map(one_block, jnp.arange(WINDOW_AMINOS // tile_portion, dtype=jnp.int32))
    return result.reshape(WINDOW_AMINOS, WINDOW_AMINOS, CP)
```

```python
import jax
import jax.numpy as jnp
from jax import lax
from jax.experimental import pallas as pl
from jax.experimental.pallas import tpu as pltpu
from jax.sharding import PartitionSpec as P

BF = jnp.bfloat16
F32 = jnp.float32
MESH = pl.DeviceIdType.MESH

SEQ = 2
RES = 640
FEAT = 256
HID = 32
CP = 128
NROW, NCOL = 8, 16
TOTAL = SEQ * NROW * NCOL
ROWS = RES // NROW
COLS = RES // NCOL
LB, LC = ROWS // 16, HID // 8
LT = LB * LC
RG = COLS // 4
LPAY, RPAY = 48, 32
CHUNK = 160


def spot(at, **step):
    size = dict(yh=2, x=4, yl=2, z=4, k=2)
    to = {a: lax.rem(at[a] + step[a], size[a]) if a in step else at[a] for a in at}
    return to["yh"] * 4 + to["x"], (to["yl"] * 4 + to["z"]) * 2 + to["k"]


def kernel(
    x_hbm, scale_ref, w1_ref, b1_ref, w2_ref, b2_ref, wf_hbm, bf_ref, pair_hbm, out_hbm,
    x_v, wf_v, pair_v, out_v, proj, pay_f, lpay, rpay, lrecv, rrecv, left, right,
    lt, rp, xk, bd, acc,
    load_sem, s1_send, s1_recv, l_send, l_recv, r_send, r_recv, k_send, k_recv,
):
    row, col = lax.axis_index("row"), lax.axis_index("col")
    at = dict(yh=row // 4, x=row % 4, yl=col // 8, z=(col // 2) % 4, k=col % 2)

    loads = [
        pltpu.make_async_copy(x_hbm, x_v, load_sem.at[0]),
        pltpu.make_async_copy(wf_hbm, wf_v, load_sem.at[1]),
        pltpu.make_async_copy(pair_hbm, pair_v, load_sem.at[2]),
    ]
    for load in loads:
        load.start()

    row_peers = [lax.rem(row + k, NROW) for k in range(1, NROW)]
    col_peers = [lax.rem(col + k, NCOL) for k in range(1, NCOL)]
    barrier = pltpu.get_barrier_semaphore()
    for r in row_peers:
        pl.semaphore_signal(barrier, inc=1, device_id=(r, col), device_id_type=MESH)
    for c in col_peers:
        pl.semaphore_signal(barrier, inc=1, device_id=(row, c), device_id_type=MESH)

    wide = lax.broadcasted_iota(jnp.int32, (512, HID), 0) // 16
    sel_l = (wide == lax.broadcasted_iota(jnp.int32, (512, HID), 1)).astype(F32)
    wide = lax.broadcasted_iota(jnp.int32, (128, HID), 0) % 32
    sel_r = (wide == lax.broadcasted_iota(jnp.int32, (128, HID), 1)).astype(F32)
    w_l = jnp.dot(sel_l.astype(BF), w1_ref[...], preferred_element_type=F32).astype(BF)
    w_r = jnp.dot(sel_r.astype(BF), w2_ref[...], preferred_element_type=F32).astype(BF)
    across = (((1,), (1,)), ((), ()))
    exact = dict(precision=lax.Precision.HIGHEST, preferred_element_type=F32)
    b_l = lax.dot_general(b1_ref[...], sel_l, across, **exact)
    b_r = lax.dot_general(b2_ref[...], sel_r, across, **exact)
    scale = scale_ref[...]

    loads[0].wait()

    def norm(i, carry):
        rows = pl.ds(pl.multiple_of(i * CHUNK, CHUNK), CHUNK)
        x = x_v[rows, :].astype(F32)
        mean = jnp.sum(x, axis=1, keepdims=True) * (1.0 / FEAT)
        dev = x - mean
        var = jnp.sum(dev * dev, axis=1, keepdims=True) * (1.0 / FEAT)
        normed = (dev * lax.rsqrt(var + 1e-5) * scale).astype(BF)
        p_l = lax.dot_general(normed, w_l, across, preferred_element_type=F32)
        for c4 in range(LC):
            proj[c4, rows, :] = p_l[:, c4 * 128 : c4 * 128 + 128]
        proj[LC, rows, :] = lax.dot_general(
            normed, w_r, across, preferred_element_type=F32
        )
        return carry

    lax.fori_loop(0, SEQ * RES // CHUNK, norm, 0)

    lane = lax.broadcasted_iota(jnp.int32, (LB, 128), 1) % 16
    for r in range(NROW):
        for s in range(SEQ):
            for c4 in range(LC):
                lanes = slice(c4 * 128, c4 * 128 + 128)
                got = proj[c4, pl.ds(s * RES + r * ROWS, LB, stride=16), :]
                for p in range(1, 16):
                    piece = proj[c4, pl.ds(s * RES + r * ROWS + p, LB, stride=16), :]
                    got = jnp.where(lane == p, piece, got)
                pay_f[pl.ds(r * LPAY + (s * LC + c4) * LB, LB), :] = got + b_l[:, lanes]
    lpay[...] = pay_f[: NROW * LPAY, :].astype(BF).reshape(NROW, LPAY, 128)

    pl.semaphore_wait(barrier, len(row_peers) + len(col_peers))
    s1_l = []
    for k, r in enumerate(row_peers):
        s1_l.append(
            pltpu.make_async_remote_copy(
                src_ref=lpay.at[r], dst_ref=lrecv.at[row],
                send_sem=s1_send.at[k], recv_sem=s1_recv.at[k],
                device_id=(r, col), device_id_type=MESH,
            )
        )
        s1_l[-1].start()
    lrecv[row] = lpay[row]

    lane = lax.broadcasted_iota(jnp.int32, (RG, 128), 1) // 32
    for c in range(NCOL):
        for s in range(SEQ):
            got = proj[LC, pl.ds(s * RES + c * COLS, RG, stride=4), :]
            for p in range(1, 4):
                piece = proj[LC, pl.ds(s * RES + c * COLS + p, RG, stride=4), :]
                got = jnp.where(lane == p, piece, got)
            pay_f[pl.ds(c * RPAY + s * RG, RG), :] = got + b_r
    rpay[...] = pay_f[: NCOL * RPAY, :].astype(BF).reshape(NCOL, RPAY, 128)
    s1_r = []
    for k, c in enumerate(col_peers):
        s1_r.append(
            pltpu.make_async_remote_copy(
                src_ref=rpay.at[c], dst_ref=rrecv.at[col],
                send_sem=s1_send.at[NROW - 1 + k], recv_sem=s1_recv.at[NROW - 1 + k],
                device_id=(row, c), device_id_type=MESH,
            )
        )
        s1_r[-1].start()
    rrecv[col] = rpay[col]

    loads[1].wait()
    bd[...] = jnp.zeros_like(bd)

    def spread(c, carry):
        rows = wf_v[pl.ds(pl.multiple_of(c * HID, HID), HID), :]
        for q in range(4):
            bd[pl.ds(pl.multiple_of(c * 128 + q * 32, 32), 32), q * 128 : q * 128 + 128] = rows
        return carry

    lax.fori_loop(0, HID, spread, 0)

    def sender(ref, sends, recvs):
        def send(n, slot, part, **step):
            block = ref.at[slot] if part is None else ref.at[slot, part]
            copy = pltpu.make_async_remote_copy(
                src_ref=block, dst_ref=block, send_sem=sends.at[n], recv_sem=recvs.at[n],
                device_id=spot(at, **step), device_id_type=MESH,
            )
            copy.start()
            return copy

        return send

    send_l = sender(left, l_send, l_recv)
    send_k = sender(left, k_send, k_recv)
    send_r = sender(right, r_send, r_recv)

    def lslot(yl, z):
        return (lax.rem(at["yl"] + yl, 2) * 4 + lax.rem(at["z"] + z, 4)) * 2 + at["k"]

    def rslot(yh, x):
        return lax.rem(at["yh"] + yh, 2) * 4 + lax.rem(at["x"] + x, 4)

    la, lb = pl.ds(0, LT // 2), pl.ds(LT // 2, LT // 2)
    ra, rb = pl.ds(0, RG // 2), pl.ds(RG // 2, RG // 2)
    lcp, rcp, kcp = {}, {}, {}

    for copy in s1_l:
        copy.wait_recv()
    pay_f[: NROW * LPAY, :] = lrecv[...].reshape(NROW * LPAY, 128).astype(F32)
    for b in range(LB):
        for c4 in range(LC):
            parts = [
                pay_f[pl.ds((s * LC + c4) * LB + b, NROW, stride=LPAY), :] for s in range(SEQ)
            ]
            left[col, b * LC + c4] = jnp.concatenate(parts, axis=0).astype(BF)
    lcp[0] = send_l(0, lslot(0, 0), None, yl=1)
    lcp[1] = send_l(1, lslot(0, 0), None, z=1)
    lcp[2] = send_l(2, lslot(0, 0), None, z=3)
    kcp[0] = send_k(0, lslot(0, 0), None, k=1)

    for copy in s1_r:
        copy.wait_recv()
    pay_f[: NCOL * RPAY, :] = rrecv[...].reshape(NCOL * RPAY, 128).astype(F32)
    for g in range(RG):
        parts = [pay_f[pl.ds(s * RG + g, NCOL, stride=RPAY), :] for s in range(SEQ)]
        right[row, g] = jnp.concatenate(parts, axis=0).astype(BF)
    rcp[0] = send_r(0, rslot(0, 0), None, yh=1)
    rcp[1] = send_r(1, rslot(0, 0), None, x=1)
    rcp[2] = send_r(2, rslot(0, 0), None, x=3)

    lcp[0].wait_recv()
    lcp[3] = send_l(3, lslot(1, 0), None, z=1)
    lcp[4] = send_l(4, lslot(1, 0), None, z=3)
    kcp[1] = send_k(1, lslot(1, 0), None, k=1)
    rcp[0].wait_recv()
    rcp[3] = send_r(3, rslot(1, 0), None, x=1)
    rcp[4] = send_r(4, rslot(1, 0), None, x=3)
    for y in range(2):
        near = 1 if y == 0 else 3
        lcp[near].wait_recv()
        lcp[5 + 2 * y] = send_l(5 + 2 * y, lslot(y, 3), la, z=1)
        kcp[2 + 2 * y] = send_k(2 + 2 * y, lslot(y, 3), None, k=1)
        rcp[near].wait_recv()
        rcp[5 + 2 * y] = send_r(5 + 2 * y, rslot(y, 3), ra, x=1)
        lcp[near + 1].wait_recv()
        lcp[6 + 2 * y] = send_l(6 + 2 * y, lslot(y, 1), lb, z=3)
        kcp[3 + 2 * y] = send_k(3 + 2 * y, lslot(y, 1), None, k=1)
        rcp[near + 1].wait_recv()
        rcp[6 + 2 * y] = send_r(6 + 2 * y, rslot(y, 1), rb, x=3)
    for y in range(2):
        lcp[5 + 2 * y].wait_recv()
        kcp[6 + 2 * y] = send_k(6 + 2 * y, lslot(y, 2), la, k=1)
        lcp[6 + 2 * y].wait_recv()
        kcp[7 + 2 * y] = send_k(7 + 2 * y, lslot(y, 2), lb, k=1)
    for y in range(2):
        rcp[5 + 2 * y].wait_recv()
        rcp[6 + 2 * y].wait_recv()

    new = lax.broadcasted_iota(jnp.int32, (TOTAL, TOTAL), 0)
    old = lax.broadcasted_iota(jnp.int32, (TOTAL, TOTAL), 1)
    perm = ((new % 8) * 32 + (new // 8) % 2 * 16 + new // 16 == old).astype(F32).astype(BF)
    for g in range(RG):
        block = right[:, g].reshape(TOTAL, 128)
        rp[:, g * 128 : g * 128 + 128] = jnp.dot(
            perm, block, preferred_element_type=F32
        ).astype(BF)

    for n in range(10):
        kcp[n].wait_recv()

    def turn(t, carry):
        lt[pl.ds(pl.multiple_of(t * 128, 128), 128), :] = jnp.transpose(
            left[:, t].reshape(TOTAL, 128)
        )
        return carry

    lax.fori_loop(0, LT, turn, 0, unroll=4)

    def outer(b, carry):
        for n in range(RG // 2):
            for h in range(2):
                x = jnp.dot(
                    lt[pl.ds(pl.multiple_of(b * 512, 512) + h * 256, 256), :],
                    rp[:, n * 256 : n * 256 + 256],
                    preferred_element_type=F32,
                ).astype(BF)
                for c in range(16):
                    for g in range(2):
                        at_row = pl.multiple_of((2 * n + g) * ROWS + b * 16, 16)
                        at_lane = (h * 16 + c) * 128
                        xk[pl.ds(at_row, 16), at_lane : at_lane + 128] = x[
                            c * 16 : c * 16 + 16, g * 128 : g * 128 + 128
                        ]
        return carry

    lax.fori_loop(0, LB, outer, 0)

    per = 5 * ROWS

    def project(m, carry):
        r = jnp.dot(
            xk[pl.ds(pl.multiple_of(m * per, per), per), :], bd[...], preferred_element_type=F32
        )
        for g in range(5):
            for q in range(4):
                acc[pl.ds(m * 20 + g * 4 + q, ROWS, stride=COLS), :] = r[
                    g * ROWS : g * ROWS + ROWS, q * 128 : q * 128 + 128
                ]
        return carry

    lax.fori_loop(0, 2, project, 0)

    loads[2].wait()
    bias = bf_ref[...]

    def finish(i, carry):
        rows = pl.ds(pl.multiple_of(i * 320, 320), 320)
        update = acc[rows, :] * (1.0 / TOTAL) + bias
        out_v[rows, :] = (pair_v[rows, :].astype(F32) + update).astype(BF)
        return carry

    lax.fori_loop(0, ROWS * COLS // 320, finish, 0)
    store = pltpu.make_async_copy(out_v, out_hbm, load_sem.at[0])
    store.start()
    for copy in s1_l + s1_r + list(lcp.values()) + list(rcp.values()) + list(kcp.values()):
        copy.wait_send()
    store.wait()


def body(x, scale, w1, b1, w2, b2, wf, bf, pair):
    vmem = pl.BlockSpec(memory_space=pltpu.VMEM)
    hbm = pl.BlockSpec(memory_space=pl.ANY)
    dma = pltpu.SemaphoreType.DMA
    n1 = NROW + NCOL - 2
    out = pl.pallas_call(
        kernel,
        out_shape=jax.ShapeDtypeStruct((ROWS * COLS, CP), BF),
        in_specs=[hbm, vmem, vmem, vmem, vmem, vmem, hbm, vmem, hbm],
        out_specs=hbm,
        scratch_shapes=[
            pltpu.VMEM((SEQ * RES, FEAT), BF),
            pltpu.VMEM((HID * HID, CP), BF),
            pltpu.VMEM((ROWS * COLS, CP), BF),
            pltpu.VMEM((ROWS * COLS, CP), BF),
            pltpu.VMEM((5, SEQ * RES, 128), F32),
            pltpu.VMEM((NCOL * RPAY, 128), F32),
            pltpu.VMEM((NROW, LPAY, 128), BF),
            pltpu.VMEM((NCOL, RPAY, 128), BF),
            pltpu.VMEM((NROW, LPAY, 128), BF),
            pltpu.VMEM((NCOL, RPAY, 128), BF),
            pltpu.VMEM((NCOL, LT, SEQ * NROW, 128), BF),
            pltpu.VMEM((NROW, RG, SEQ * NCOL, 128), BF),
            pltpu.VMEM((ROWS * HID, TOTAL), BF),
            pltpu.VMEM((TOTAL, COLS * HID), BF),
            pltpu.VMEM((RG * ROWS, HID * 128), BF),
            pltpu.VMEM((HID * 128, 4 * CP), BF),
            pltpu.VMEM((ROWS * COLS, CP), F32),
            dma((3,)), dma((n1,)), dma((n1,)),
            dma((9,)), dma((9,)), dma((9,)), dma((9,)), dma((10,)), dma((10,)),
        ],
        compiler_params=pltpu.CompilerParams(
            collective_id=0, has_side_effects=True, vmem_limit_bytes=56 * 2**20
        ),
    )(
        x.reshape(SEQ * RES, FEAT), scale.reshape(1, FEAT), w1.T, b1.reshape(1, HID),
        w2.T, b2.reshape(1, HID), wf, bf.reshape(1, CP), pair.reshape(ROWS * COLS, CP),
    )
    return out.reshape(ROWS, COLS, CP)


def solution(mesh):
    return jax.shard_map(
        body,
        mesh=mesh,
        in_specs=(P(("row", "col"), None, None), P(), P(), P(), P(), P(), P(), P(), P("row", "col", None)),
        out_specs=P("row", "col", None),
        check_vma=False,
    )
```

```python
import jax
import jax.numpy as jnp
from jax import lax
from jax.experimental import pallas as pl
from jax.experimental.pallas import tpu as pltpu
from jax.sharding import PartitionSpec as P

BF = jnp.bfloat16
F32 = jnp.float32
MESH = pl.DeviceIdType.MESH

SEQ = 2
RES = 640
FEAT = 256
HID = 32
CP = 128
NROW, NCOL = 8, 16
TOTAL = SEQ * NROW * NCOL
ROWS = RES // NROW
COLS = RES // NCOL
LB, LC = ROWS // 16, HID // 8
LT = LB * LC
RG = COLS // 4
PARTS = ((0, 3), (3, 5))
LPAY, RPAY = 48, 32
CHUNK = 160


def spot(at, **step):
    size = dict(yh=2, x=4, yl=2, z=4, k=2)
    to = {a: lax.rem(at[a] + step[a], size[a]) if a in step else at[a] for a in at}
    return to["yh"] * 4 + to["x"], (to["yl"] * 4 + to["z"]) * 2 + to["k"]


def kernel(
    x_hbm, scale_hbm, w1_hbm, b1_hbm, w2_hbm, b2_hbm, wf_hbm, bf_hbm, out_ref,
    x_v, scale_ref, w1_ref, b1_ref, w2_ref, b2_ref, wf_v, bf_ref, proj, pay_f, lpay, rpay, lrecv, rrecv, left, right,
    lt, rp, xk, bd,
    load_sem, s1_send, s1_recv, l_send, l_recv, r_send, r_recv, k_send, k_recv,
):
    row, col = lax.axis_index("row"), lax.axis_index("col")
    at = dict(yh=row // 4, x=row % 4, yl=col // 8, z=(col // 2) % 4, k=col % 2)

    loads = [
        pltpu.make_async_copy(source, held, load_sem.at[n])
        for n, (source, held) in enumerate((
            (w1_hbm, w1_ref), (w2_hbm, w2_ref), (b1_hbm, b1_ref), (b2_hbm, b2_ref),
            (scale_hbm, scale_ref), (x_hbm, x_v), (wf_hbm, wf_v), (bf_hbm, bf_ref),
        ))
    ]
    for load in loads:
        load.start()

    row_peers = [lax.rem(row + k, NROW) for k in range(1, NROW)]
    col_peers = [lax.rem(col + k, NCOL) for k in range(1, NCOL)]
    barrier = pltpu.get_barrier_semaphore()
    for r in row_peers:
        pl.semaphore_signal(barrier, inc=1, device_id=(r, col), device_id_type=MESH)
    for c in col_peers:
        pl.semaphore_signal(barrier, inc=1, device_id=(row, c), device_id_type=MESH)

    for load in loads[:5]:
        load.wait()
    wide = lax.broadcasted_iota(jnp.int32, (512, HID), 0) // 16
    sel_l = (wide == lax.broadcasted_iota(jnp.int32, (512, HID), 1)).astype(F32)
    wide = lax.broadcasted_iota(jnp.int32, (128, HID), 0) % 32
    sel_r = (wide == lax.broadcasted_iota(jnp.int32, (128, HID), 1)).astype(F32)
    w_l = jnp.dot(sel_l.astype(BF), w1_ref[...], preferred_element_type=F32).astype(BF)
    w_r = jnp.dot(sel_r.astype(BF), w2_ref[...], preferred_element_type=F32).astype(BF)
    across = (((1,), (1,)), ((), ()))
    exact = dict(precision=lax.Precision.HIGHEST, preferred_element_type=F32)
    b_l = lax.dot_general(b1_ref[...], sel_l, across, **exact)
    b_r = lax.dot_general(b2_ref[...], sel_r, across, **exact)
    scale = scale_ref[...]

    loads[5].wait()

    def norm(i, carry):
        rows = pl.ds(pl.multiple_of(i * CHUNK, CHUNK), CHUNK)
        x = x_v[rows, :].astype(F32)
        mean = jnp.sum(x, axis=1, keepdims=True) * (1.0 / FEAT)
        dev = x - mean
        var = jnp.sum(dev * dev, axis=1, keepdims=True) * (1.0 / FEAT)
        normed = (dev * lax.rsqrt(var + 1e-5) * scale).astype(BF)
        p_l = lax.dot_general(normed, w_l, across, preferred_element_type=F32)
        for c4 in range(LC):
            proj[c4, rows, :] = p_l[:, c4 * 128 : c4 * 128 + 128]
        proj[LC, rows, :] = lax.dot_general(
            normed, w_r, across, preferred_element_type=F32
        )
        return carry

    lax.fori_loop(0, SEQ * RES // CHUNK, norm, 0, unroll=4)

    lane = lax.broadcasted_iota(jnp.int32, (LB, 128), 1) % 16
    for r in range(NROW):
        for s in range(SEQ):
            for c4 in range(LC):
                lanes = slice(c4 * 128, c4 * 128 + 128)
                got = proj[c4, pl.ds(s * RES + r * ROWS, LB, stride=16), :]
                for p in range(1, 16):
                    piece = proj[c4, pl.ds(s * RES + r * ROWS + p, LB, stride=16), :]
                    got = jnp.where(lane == p, piece, got)
                pay_f[pl.ds(r * LPAY + (s * LC + c4) * LB, LB), :] = got + b_l[:, lanes]
    lpay[...] = pay_f[: NROW * LPAY, :].astype(BF).reshape(NROW, LPAY, 128)

    pl.semaphore_wait(barrier, len(row_peers) + len(col_peers))
    s1_l = []
    for k, r in enumerate(row_peers):
        s1_l.append(
            pltpu.make_async_remote_copy(
                src_ref=lpay.at[r], dst_ref=lrecv.at[row],
                send_sem=s1_send.at[k], recv_sem=s1_recv.at[k],
                device_id=(r, col), device_id_type=MESH,
            )
        )
        s1_l[-1].start()
    lrecv[row] = lpay[row]

    lane = lax.broadcasted_iota(jnp.int32, (RG, 128), 1) // 32
    for c in range(NCOL):
        for s in range(SEQ):
            got = proj[LC, pl.ds(s * RES + c * COLS, RG, stride=4), :]
            for p in range(1, 4):
                piece = proj[LC, pl.ds(s * RES + c * COLS + p, RG, stride=4), :]
                got = jnp.where(lane == p, piece, got)
            pay_f[pl.ds(c * RPAY + s * RG, RG), :] = got + b_r
    rpay[...] = pay_f[: NCOL * RPAY, :].astype(BF).reshape(NCOL, RPAY, 128)
    s1_r = []
    for k, c in enumerate(col_peers):
        s1_r.append(
            pltpu.make_async_remote_copy(
                src_ref=rpay.at[c], dst_ref=rrecv.at[col],
                send_sem=s1_send.at[NROW - 1 + k], recv_sem=s1_recv.at[NROW - 1 + k],
                device_id=(row, c), device_id_type=MESH,
            )
        )
        s1_r[-1].start()
    rrecv[col] = rpay[col]

    loads[6].wait()
    loads[7].wait()
    bd[...] = jnp.zeros_like(bd)

    def spread(c, carry):
        rows = wf_v[pl.ds(pl.multiple_of(c * HID, HID), HID), :]
        for q in range(4):
            bd[pl.ds(pl.multiple_of(c * 128 + q * 32, 32), 32), q * 128 : q * 128 + 128] = rows
        return carry

    lax.fori_loop(0, HID, spread, 0)

    me_k, me_l = at["k"], at["yl"] * 4 + at["z"]
    sends_l, sends_r, sends_k = {}, {}, {}

    def send_l(part, y, way, **step):
        lo, hi = PARTS[part]
        slot = lax.rem(at["yl"] + y, 2) * 4 + at["z"]
        block = left.at[pl.ds(lo, hi - lo), me_k, slot]
        n = len(sends_l)
        copy = pltpu.make_async_remote_copy(
            src_ref=block, dst_ref=block, send_sem=l_send.at[n], recv_sem=l_recv.at[n],
            device_id=spot(at, **step), device_id_type=MESH,
        )
        copy.start()
        sends_l[part, y, way] = copy

    def send_r(y, way, **step):
        block = right.at[lax.rem(at["yh"] + y, 2) * 4 + at["x"]]
        n = len(sends_r)
        copy = pltpu.make_async_remote_copy(
            src_ref=block, dst_ref=block, send_sem=r_send.at[n], recv_sem=r_recv.at[n],
            device_id=spot(at, **step), device_id_type=MESH,
        )
        copy.start()
        sends_r[y, way] = copy

    def send_k(part):
        lo, hi = PARTS[part]
        block = left.at[pl.ds(lo, hi - lo), me_k]
        copy = pltpu.make_async_remote_copy(
            src_ref=block, dst_ref=block, send_sem=k_send.at[part], recv_sem=k_recv.at[part],
            device_id=spot(at, k=1), device_id_type=MESH,
        )
        copy.start()
        sends_k[part] = copy

    def ring_l(part, y):
        for step in (1, 3, 2):
            send_l(part, y, step, z=step)

    def ring_r(y):
        for step in (1, 3, 2):
            send_r(y, step, x=step)

    def arrived_l(part):
        for y in range(2):
            for step in (1, 3, 2):
                sends_l[part, y, step].wait_recv()
        send_k(part)

    for copy in s1_l:
        copy.wait_recv()
    pay_f[: NROW * LPAY, :] = lrecv[...].reshape(NROW * LPAY, 128).astype(F32)
    for b in range(LB):
        for c4 in range(LC):
            parts = [
                pay_f[pl.ds((s * LC + c4) * LB + b, NROW, stride=LPAY), :] for s in range(SEQ)
            ]
            left[b, me_k, me_l, c4] = jnp.concatenate(parts, axis=0).astype(BF)
    send_l(0, 0, "y", yl=1)
    ring_l(0, 0)

    for copy in s1_r:
        copy.wait_recv()
    pay_f[: NCOL * RPAY, :] = rrecv[...].reshape(NCOL * RPAY, 128).astype(F32)
    for g in range(RG):
        parts = [pay_f[pl.ds(s * RG + g, NCOL, stride=RPAY), :] for s in range(SEQ)]
        right[row, g] = jnp.concatenate(parts, axis=0).astype(BF)
    send_r(0, "y", yh=1)
    ring_r(0)

    sends_l[0, 0, "y"].wait_recv()
    ring_l(0, 1)
    send_l(1, 0, "y", yl=1)
    sends_r[0, "y"].wait_recv()
    ring_r(1)
    ring_l(1, 0)
    sends_l[1, 0, "y"].wait_recv()
    ring_l(1, 1)

    arrived_l(0)
    for y in range(2):
        for step in (1, 3, 2):
            sends_r[y, step].wait_recv()

    new = lax.broadcasted_iota(jnp.int32, (TOTAL, TOTAL), 0)
    old = lax.broadcasted_iota(jnp.int32, (TOTAL, TOTAL), 1)
    from_old = new % 8 * 32 + new // 8 % 2 * 16 + new // 16 % 8 * 2 + new // 128
    perm = (from_old == old).astype(F32).astype(BF)
    for g in range(RG):
        block = right[:, g].reshape(TOTAL, 128)
        rp[:, g * 128 : g * 128 + 128] = jnp.dot(
            perm, block, preferred_element_type=F32
        ).astype(BF)

    def outer(b, carry):
        for c4 in range(LC):
            lt[pl.ds(pl.multiple_of(b * 512, 512) + c4 * 128, 128), :] = jnp.transpose(
                left[b, :, :, c4].reshape(TOTAL, 128)
            )
        for n in range(RG // 2):
            for h in range(2):
                x = jnp.dot(
                    lt[pl.ds(pl.multiple_of(b * 512, 512) + h * 256, 256), :],
                    rp[:, n * 256 : n * 256 + 256],
                    preferred_element_type=F32,
                ).astype(BF)
                for c in range(16):
                    for g in range(2):
                        at_row = pl.multiple_of(b * 16 * RG, 16) + (2 * n + g) * 16
                        at_lane = (h * 16 + c) * 128
                        xk[pl.ds(at_row, 16), at_lane : at_lane + 128] = x[
                            c * 16 : c * 16 + 16, g * 128 : g * 128 + 128
                        ]
        return carry

    def project(part):
        lo, hi = PARTS[part]
        r = jnp.dot(
            xk[lo * 16 * RG : hi * 16 * RG, :], bd[...], preferred_element_type=F32
        ) * (1.0 / TOTAL)
        for b in range(hi - lo):
            for g in range(RG):
                for q in range(4):
                    at_row = (lo + b) * 16 * COLS + g * 4 + q
                    from_row = (b * RG + g) * 16
                    out_ref[pl.ds(at_row, 16, stride=COLS), :] = r[
                        from_row : from_row + 16, q * 128 : q * 128 + 128
                    ] + bf_ref[...]

    sends_k[0].wait_recv()
    lax.fori_loop(*PARTS[0], outer, 0)
    arrived_l(1)
    project(0)
    sends_k[1].wait_recv()
    lax.fori_loop(*PARTS[1], outer, 0)
    project(1)

    sent = s1_l + s1_r + list(sends_l.values()) + list(sends_r.values()) + list(sends_k.values())
    for copy in sent:
        copy.wait_send()


def body(x, scale, w1, b1, w2, b2, wf, bf, pair):
    vmem = pl.BlockSpec(memory_space=pltpu.VMEM)
    hbm = pl.BlockSpec(memory_space=pltpu.HBM)
    dma = pltpu.SemaphoreType.DMA
    n1 = NROW + NCOL - 2
    acc = pl.pallas_call(
        kernel,
        out_shape=pltpu.VMEM((ROWS * COLS, CP), F32),
        in_specs=[hbm] * 8,
        out_specs=vmem,
        scratch_shapes=[
            pltpu.VMEM((SEQ * RES, FEAT), BF),
            pltpu.VMEM((1, FEAT), F32),
            pltpu.VMEM((HID, FEAT), BF),
            pltpu.VMEM((1, HID), F32),
            pltpu.VMEM((HID, FEAT), BF),
            pltpu.VMEM((1, HID), F32),
            pltpu.VMEM((HID * HID, CP), BF),
            pltpu.VMEM((1, CP), F32),
            pltpu.VMEM((5, SEQ * RES, 128), F32),
            pltpu.VMEM((NCOL * RPAY, 128), F32),
            pltpu.VMEM((NROW, LPAY, 128), BF),
            pltpu.VMEM((NCOL, RPAY, 128), BF),
            pltpu.VMEM((NROW, LPAY, 128), BF),
            pltpu.VMEM((NCOL, RPAY, 128), BF),
            pltpu.VMEM((LB, 2, 8, LC, SEQ * NROW, 128), BF),
            pltpu.VMEM((NROW, RG, SEQ * NCOL, 128), BF),
            pltpu.VMEM((ROWS * HID, TOTAL), BF),
            pltpu.VMEM((TOTAL, COLS * HID), BF),
            pltpu.VMEM((RG * ROWS, HID * 128), BF),
            pltpu.VMEM((HID * 128, 4 * CP), BF),
            dma((8,)), dma((n1,)), dma((n1,)),
            dma((14,)), dma((14,)), dma((7,)), dma((7,)), dma((2,)), dma((2,)),
        ],
        compiler_params=pltpu.CompilerParams(
            collective_id=0, has_side_effects=True, vmem_limit_bytes=56 * 2**20
        ),
    )(
        x.reshape(SEQ * RES, FEAT), scale.reshape(1, FEAT), w1.T, b1.reshape(1, HID),
        w2.T, b2.reshape(1, HID), wf, bf.reshape(1, CP),
    )
    return (pair.astype(F32) + acc.reshape(ROWS, COLS, CP)).astype(BF)


def solution(mesh):
    return jax.shard_map(
        body,
        mesh=mesh,
        in_specs=(P(("row", "col"), None, None), P(), P(), P(), P(), P(), P(), P(), P("row", "col", None)),
        out_specs=P("row", "col", None),
        check_vma=False,
    )
```

```python
import jax
import jax.numpy as jnp
from jax import lax
from jax.experimental import pallas as pl
from jax.experimental.pallas import tpu as pltpu
from jax.sharding import PartitionSpec as P

BF = jnp.bfloat16
F32 = jnp.float32
MESH = pl.DeviceIdType.MESH

SEQ = 2
RES = 640
FEAT = 256
HID = 32
CP = 128
NROW, NCOL = 8, 16
TOTAL = SEQ * NROW * NCOL
ROWS = RES // NROW
COLS = RES // NCOL
LB, LC = ROWS // 16, HID // 8
LT = LB * LC
RG = COLS // 4
RING = (2, 1, 3)
PARTS = ((0, 3), (3, 5))
LPAY, RPAY = 48, 32
CHUNK = 320


def spot(at, **step):
    size = dict(yh=2, x=4, yl=2, z=4, k=2)
    to = {a: lax.rem(at[a] + step[a], size[a]) if a in step else at[a] for a in at}
    return to["yh"] * 4 + to["x"], (to["yl"] * 4 + to["z"]) * 2 + to["k"]


def kernel(
    x_hbm, scale_hbm, w1_hbm, b1_hbm, w2_hbm, b2_hbm, wf_hbm, bf_hbm, out_ref,
    x_v, scale_ref, w1_ref, b1_ref, w2_ref, b2_ref, wf_v, bf_ref, proj, pay_f, lpay, rpay, lrecv, rrecv, left, right,
    lt, rp, xk, bd,
    load_sem, s1_send, s1_recv, l_send, l_recv, r_send, r_recv, k_send, k_recv,
):
    row, col = lax.axis_index("row"), lax.axis_index("col")
    at = dict(yh=row // 4, x=row % 4, yl=col // 8, z=(col // 2) % 4, k=col % 2)

    loads = [
        pltpu.make_async_copy(source, held, load_sem.at[n])
        for n, (source, held) in enumerate((
            (w1_hbm, w1_ref), (w2_hbm, w2_ref), (b1_hbm, b1_ref), (b2_hbm, b2_ref),
            (scale_hbm, scale_ref), (x_hbm, x_v), (wf_hbm, wf_v), (bf_hbm, bf_ref),
        ))
    ]
    for load in loads:
        load.start()

    other = lax.rem(col + NCOL // 2, NCOL)
    l_peers = [(k, lax.rem(row + k, NROW), c) for c in (col, other) for k in range(NROW)][1:]
    r_peers = [lax.rem(col + k, NCOL) for k in range(1, NCOL)]
    greet = [(r, c) for k, r, c in l_peers if k > 0] + [(row, c) for c in r_peers]
    barrier = pltpu.get_barrier_semaphore()
    for peer in greet:
        pl.semaphore_signal(barrier, inc=1, device_id=peer, device_id_type=MESH)

    for load in loads[:5]:
        load.wait()
    wide = lax.broadcasted_iota(jnp.int32, (512, HID), 0) // 16
    wide = wide % 16 * 2 + wide // 16
    sel_l = (wide == lax.broadcasted_iota(jnp.int32, (512, HID), 1)).astype(F32)
    wide = lax.broadcasted_iota(jnp.int32, (128, HID), 0) % 32
    sel_r = (wide == lax.broadcasted_iota(jnp.int32, (128, HID), 1)).astype(F32)
    w_l = jnp.dot(sel_l.astype(BF), w1_ref[...], preferred_element_type=F32).astype(BF)
    w_r = jnp.dot(sel_r.astype(BF), w2_ref[...], preferred_element_type=F32).astype(BF)
    across = (((1,), (1,)), ((), ()))
    exact = dict(precision=lax.Precision.HIGHEST, preferred_element_type=F32)
    b_l = lax.dot_general(b1_ref[...], sel_l, across, **exact)
    b_r = lax.dot_general(b2_ref[...], sel_r, across, **exact)
    scale = scale_ref[...]

    loads[5].wait()

    def norm(i):
        rows = pl.ds(i * CHUNK, CHUNK)
        x = x_v[rows, :].astype(F32)
        mean = jnp.sum(x, axis=1, keepdims=True) * (1.0 / FEAT)
        dev = x - mean
        var = jnp.sum(dev * dev, axis=1, keepdims=True) * (1.0 / FEAT)
        normed = (dev * lax.rsqrt(var + 1e-5) * scale).astype(BF)
        p_l = lax.dot_general(normed, w_l, across, preferred_element_type=F32)
        for c4 in range(LC):
            proj[c4, rows, :] = p_l[:, c4 * 128 : c4 * 128 + 128]
        proj[LC, rows, :] = lax.dot_general(
            normed, w_r, across, preferred_element_type=F32
        )

    for i in range(SEQ * RES // CHUNK):
        norm(i)

    lane = lax.broadcasted_iota(jnp.int32, (RES // 4, 128), 1) // 32
    for s in range(SEQ):
        got = proj[LC, pl.ds(s * RES, RES // 4, stride=4), :]
        for p in range(1, 4):
            piece = proj[LC, pl.ds(s * RES + p, RES // 4, stride=4), :]
            got = jnp.where(lane == p, piece, got)
        got = got + b_r
        for c in range(NCOL):
            pay_f[pl.ds(c * RPAY + s * RG, RG), :] = got[c * RG : c * RG + RG]
    rpay[...] = pay_f[: NCOL * RPAY, :].astype(BF).reshape(NCOL, RPAY, 128)
    pl.semaphore_wait(barrier, len(greet))
    s1_r = []
    for n, c in enumerate(r_peers):
        n += len(l_peers)
        s1_r.append(
            pltpu.make_async_remote_copy(
                src_ref=rpay.at[c], dst_ref=rrecv.at[col],
                send_sem=s1_send.at[n], recv_sem=s1_recv.at[n],
                device_id=(row, c), device_id_type=MESH,
            )
        )
        s1_r[-1].start()
    rrecv[col] = rpay[col]

    lane = lax.broadcasted_iota(jnp.int32, (RES // 16, 128), 1) % 16
    for s in range(SEQ):
        for c4 in range(LC):
            got = proj[c4, pl.ds(s * RES, RES // 16, stride=16), :]
            for p in range(1, 16):
                piece = proj[c4, pl.ds(s * RES + p, RES // 16, stride=16), :]
                got = jnp.where(lane == p, piece, got)
            got = got + b_l[:, c4 * 128 : c4 * 128 + 128]
            for r in range(NROW):
                pay_f[pl.ds(r * LPAY + (s * LC + c4) * LB, LB), :] = got[r * LB : r * LB + LB]
    lpay[...] = pay_f[: NROW * LPAY, :].astype(BF).reshape(NROW, LPAY, 128)
    s1_l = []
    for n, (_, r, c) in enumerate(l_peers):
        s1_l.append(
            pltpu.make_async_remote_copy(
                src_ref=lpay.at[r], dst_ref=lrecv.at[at["yl"], row],
                send_sem=s1_send.at[n], recv_sem=s1_recv.at[n],
                device_id=(r, c), device_id_type=MESH,
            )
        )
        s1_l[-1].start()
    lrecv[at["yl"], row] = lpay[row]

    loads[6].wait()
    loads[7].wait()
    bd[...] = jnp.zeros_like(bd)

    def spread(p, carry):
        for half in range(2):
            for place in range(2):
                c = 2 * p + (place ^ half)
                rows = wf_v[pl.ds(pl.multiple_of(c * HID, HID), HID), :]
                for q in range(2):
                    at_row = pl.multiple_of(p * 128 + place * 64 + q * HID, HID)
                    bd[half, pl.ds(at_row, HID), q * 128 : q * 128 + 128] = rows
        return carry

    lax.fori_loop(0, HID // 2, spread, 0, unroll=4)

    k, yl, z = at["k"], at["yl"], at["z"]
    sends_l, sends_r, sends_k = {}, {}, {}

    def copy_out(ref, sends, sems, key, step):
        n = len(sends)
        copy = pltpu.make_async_remote_copy(
            src_ref=ref, dst_ref=ref, send_sem=sems[0].at[n], recv_sem=sems[1].at[n],
            device_id=spot(at, **step), device_id_type=MESH,
        )
        copy.start()
        sends[key] = copy

    def tiles(part, away):
        lo, hi = PARTS[part]
        return left.at[pl.ds(lo, hi - lo), k, pl.ds(lax.rem(z + away, 4) * 2, 2)]

    def ring_l(part):
        for step in RING:
            copy_out(tiles(part, 0), sends_l, (l_send, l_recv), (part, step), dict(z=step))

    def other_core(part, away):
        copy_out(tiles(part, away), sends_k, (k_send, k_recv), (part, away), dict(k=1))

    def arrived_l(part):
        for step in RING:
            sends_l[part, step].wait_recv()
            other_core(part, (4 - step) % 4)

    def right_of(y):
        return right.at[lax.rem(at["yh"] + y, 2) * 4 + at["x"]]

    def ring_r(y):
        for step in RING:
            copy_out(right_of(y), sends_r, (r_send, r_recv), (y, step), dict(x=step))

    for copy in s1_r:
        copy.wait_recv()
    pay_f[: NCOL * RPAY, :] = rrecv[...].reshape(NCOL * RPAY, 128).astype(F32)
    for g in range(RG):
        parts = [pay_f[pl.ds(s * RG + g, NCOL, stride=RPAY), :] for s in range(SEQ)]
        right[row, g] = jnp.concatenate(parts, axis=0).astype(BF)
    copy_out(right_of(0), sends_r, (r_send, r_recv), "y", dict(yh=1))
    ring_r(0)

    for copy in s1_l:
        copy.wait_recv()
    for y in range(2):
        pay_f[: NROW * LPAY, :] = lrecv[y].reshape(NROW * LPAY, 128).astype(F32)
        for b in range(LB):
            for c4 in range(LC):
                parts = [
                    pay_f[pl.ds((s * LC + c4) * LB + b, NROW, stride=LPAY), :] for s in range(SEQ)
                ]
                left[b, k, z * 2 + y, c4] = jnp.concatenate(parts, axis=0).astype(BF)
    ring_l(0)
    other_core(0, 0)
    other_core(1, 0)

    sends_r["y"].wait_recv()
    ring_r(1)
    ring_l(1)
    arrived_l(0)
    for y in range(2):
        for step in RING:
            sends_r[y, step].wait_recv()

    new = lax.broadcasted_iota(jnp.int32, (TOTAL, TOTAL), 0)
    old = lax.broadcasted_iota(jnp.int32, (TOTAL, TOTAL), 1)
    from_col = new // 16 % 2 * 8 + new // 32 % 4 * 2 + new // 128
    perm = (new % 8 * 32 + new // 8 % 2 * 16 + from_col == old).astype(F32).astype(BF)
    for g in range(RG):
        block = jnp.dot(
            perm, right[:, g].reshape(TOTAL, 128), preferred_element_type=F32
        ).astype(BF)
        at_lane = g * 128
        rp[0, :, at_lane : at_lane + 128] = block
        rp[1, :, at_lane : at_lane + 64] = block[:, 64:]
        rp[1, :, at_lane + 64 : at_lane + 128] = block[:, :64]

    low = lax.broadcasted_iota(jnp.int32, (256, 256), 1) % 128 < 64

    def outer(b):
        for c4 in range(LC):
            lt[b * 512 + c4 * 128 : b * 512 + c4 * 128 + 128, :] = jnp.transpose(
                left[b, :, :, c4].reshape(TOTAL, 128)
            )
        for n in range(RG // 2):
            even, odd = (
                jnp.dot(
                    lt[b * 512 + h * 256 : b * 512 + h * 256 + 256, :],
                    rp[h, :, n * 256 : n * 256 + 256],
                    preferred_element_type=F32,
                ).astype(BF)
                for h in range(2)
            )
            for half, x in enumerate((jnp.where(low, even, odd), jnp.where(low, odd, even))):
                for p in range(HID // 2):
                    for g in range(2):
                        at_row = (b * RG + 2 * n + g) * 16
                        xk[half, at_row : at_row + 16, p * 128 : p * 128 + 128] = x[
                            p * 16 : p * 16 + 16, g * 128 : g * 128 + 128
                        ]

    def project(part):
        lo, hi = PARTS[part]
        for half in range(2):
            r = jnp.dot(
                xk[half, lo * 16 * RG : hi * 16 * RG, :], bd[half], preferred_element_type=F32
            ) * (1.0 / TOTAL)
            for b in range(hi - lo):
                for g in range(RG):
                    for q in range(2):
                        at_row = (lo + b) * 16 * COLS + g * 4 + half * 2 + q
                        from_row = (b * RG + g) * 16
                        out_ref[pl.ds(at_row, 16, stride=COLS), :] = r[
                            from_row : from_row + 16, q * 128 : q * 128 + 128
                        ] + bf_ref[...]

    def from_core(part):
        for away in range(4):
            sends_k[part, away].wait_recv()

    from_core(0)
    for b in range(*PARTS[0]):
        outer(b)
    arrived_l(1)
    project(0)
    from_core(1)
    for b in range(*PARTS[1]):
        outer(b)
    project(1)

    for sends in (sends_l, sends_r, sends_k):
        for copy in sends.values():
            copy.wait_send()
    for copy in s1_l + s1_r:
        copy.wait_send()


def body(x, scale, w1, b1, w2, b2, wf, bf, pair):
    vmem = pl.BlockSpec(memory_space=pltpu.VMEM)
    hbm = pl.BlockSpec(memory_space=pltpu.HBM)
    dma = pltpu.SemaphoreType.DMA
    n1 = 2 * NROW - 1 + NCOL - 1
    acc = pl.pallas_call(
        kernel,
        out_shape=pltpu.VMEM((ROWS * COLS, CP), F32),
        in_specs=[hbm] * 8,
        out_specs=vmem,
        scratch_shapes=[
            pltpu.VMEM((SEQ * RES, FEAT), BF),
            pltpu.VMEM((1, FEAT), F32),
            pltpu.VMEM((HID, FEAT), BF),
            pltpu.VMEM((1, HID), F32),
            pltpu.VMEM((HID, FEAT), BF),
            pltpu.VMEM((1, HID), F32),
            pltpu.VMEM((HID * HID, CP), BF),
            pltpu.VMEM((1, CP), F32),
            pltpu.VMEM((5, SEQ * RES, 128), F32),
            pltpu.VMEM((NCOL * RPAY, 128), F32),
            pltpu.VMEM((NROW, LPAY, 128), BF),
            pltpu.VMEM((NCOL, RPAY, 128), BF),
            pltpu.VMEM((2, NROW, LPAY, 128), BF),
            pltpu.VMEM((NCOL, RPAY, 128), BF),
            pltpu.VMEM((LB, 2, 8, LC, SEQ * NROW, 128), BF),
            pltpu.VMEM((NROW, RG, SEQ * NCOL, 128), BF),
            pltpu.VMEM((ROWS * HID, TOTAL), BF),
            pltpu.VMEM((2, TOTAL, COLS * HID), BF),
            pltpu.VMEM((2, RG * ROWS, HID * 64), BF),
            pltpu.VMEM((2, HID * 64, 2 * CP), BF),
            dma((8,)), dma((n1,)), dma((n1,)),
            dma((6,)), dma((6,)), dma((7,)), dma((7,)), dma((8,)), dma((8,)),
        ],
        compiler_params=pltpu.CompilerParams(
            collective_id=0, has_side_effects=True, vmem_limit_bytes=56 * 2**20
        ),
    )(
        x.reshape(SEQ * RES, FEAT), scale.reshape(1, FEAT), w1.T, b1.reshape(1, HID),
        w2.T, b2.reshape(1, HID), wf, bf.reshape(1, CP),
    )
    return (pair.astype(F32) + acc.reshape(ROWS, COLS, CP)).astype(BF)


def solution(mesh):
    return jax.shard_map(
        body,
        mesh=mesh,
        in_specs=(P(("row", "col"), None, None), P(), P(), P(), P(), P(), P(), P(), P("row", "col", None)),
        out_specs=P("row", "col", None),
        check_vma=False,
    )
```

```python
import jax
import jax.numpy as jnp
from jax import lax
from jax.experimental import pallas as pl
from jax.experimental.pallas import tpu as pltpu
from jax.sharding import PartitionSpec as P

BF = jnp.bfloat16
F32 = jnp.float32
MESH = pl.DeviceIdType.MESH

SEQ = 2
RES = 640
FEAT = 256
HID = 32
CP = 128
NROW, NCOL = 8, 16
TOTAL = SEQ * NROW * NCOL
ROWS = RES // NROW
COLS = RES // NCOL
LB, LC = ROWS // 16, HID // 8
LT = LB * LC
RG = COLS // 4
PARTS = ((0, 2), (2, 4), (4, 5))
LPAY, RPAY = 48, 32
CHUNK = 320


def spot(at, **step):
    size = dict(yh=2, x=4, yl=2, z=4, k=2)
    to = {a: lax.rem(at[a] + step[a], size[a]) if a in step else at[a] for a in at}
    return to["yh"] * 4 + to["x"], (to["yl"] * 4 + to["z"]) * 2 + to["k"]


def kernel(
    x_hbm, scale_hbm, w1_hbm, b1_hbm, w2_hbm, b2_hbm, wf_hbm, bf_hbm, pair_hbm, out_ref,
    x_v, scale_ref, w1_ref, b1_ref, w2_ref, b2_ref, wf_v, bf_ref, pair_v, acc, proj, pay_f, lpay, rpay, lrecv, rrecv, left, right,
    lt, rp, xk, bd,
    load_sem, s1_send, s1_recv, l_send, l_recv, r_send, r_recv, k_send, k_recv,
):
    row, col = lax.axis_index("row"), lax.axis_index("col")
    at = dict(yh=row // 4, x=row % 4, yl=col // 8, z=(col // 2) % 4, k=col % 2)

    loads = [
        pltpu.make_async_copy(source, held, load_sem.at[n])
        for n, (source, held) in enumerate((
            (w1_hbm, w1_ref), (w2_hbm, w2_ref), (b1_hbm, b1_ref), (b2_hbm, b2_ref),
            (scale_hbm, scale_ref), (x_hbm, x_v), (wf_hbm, wf_v), (bf_hbm, bf_ref),
            (pair_hbm, pair_v),
        ))
    ]
    for load in loads:
        load.start()

    other = lax.rem(col + NCOL // 2, NCOL)
    l_peers = [(k, lax.rem(row + k, NROW), c) for c in (col, other) for k in range(NROW)][1:]
    r_peers = [lax.rem(col + k, NCOL) for k in range(1, NCOL)]
    greet = [(r, c) for k, r, c in l_peers if k > 0] + [(row, c) for c in r_peers]
    barrier = pltpu.get_barrier_semaphore()
    for peer in greet:
        pl.semaphore_signal(barrier, inc=1, device_id=peer, device_id_type=MESH)

    for load in loads[:5]:
        load.wait()
    wide = lax.broadcasted_iota(jnp.int32, (512, HID), 0) // 16
    wide = wide % 16 * 2 + wide // 16
    sel_l = (wide == lax.broadcasted_iota(jnp.int32, (512, HID), 1)).astype(F32)
    wide = lax.broadcasted_iota(jnp.int32, (128, HID), 0) % 32
    sel_r = (wide == lax.broadcasted_iota(jnp.int32, (128, HID), 1)).astype(F32)
    w_l = jnp.dot(sel_l.astype(BF), w1_ref[...], preferred_element_type=F32).astype(BF)
    w_r = jnp.dot(sel_r.astype(BF), w2_ref[...], preferred_element_type=F32).astype(BF)
    across = (((1,), (1,)), ((), ()))
    exact = dict(precision=lax.Precision.HIGHEST, preferred_element_type=F32)
    b_l = lax.dot_general(b1_ref[...], sel_l, across, **exact)
    b_r = lax.dot_general(b2_ref[...], sel_r, across, **exact)
    scale = scale_ref[...]

    loads[5].wait()

    def norm(i):
        rows = pl.ds(i * CHUNK, CHUNK)
        x = x_v[rows, :].astype(F32)
        mean = jnp.sum(x, axis=1, keepdims=True) * (1.0 / FEAT)
        dev = x - mean
        var = jnp.sum(dev * dev, axis=1, keepdims=True) * (1.0 / FEAT)
        normed = (dev * lax.rsqrt(var + 1e-5) * scale).astype(BF)
        p_l = lax.dot_general(normed, w_l, across, preferred_element_type=F32)
        for c4 in range(LC):
            proj[c4, rows, :] = p_l[:, c4 * 128 : c4 * 128 + 128]
        proj[LC, rows, :] = lax.dot_general(
            normed, w_r, across, preferred_element_type=F32
        )

    for i in range(SEQ * RES // CHUNK):
        norm(i)

    lane = lax.broadcasted_iota(jnp.int32, (RES // 4, 128), 1) // 32
    for s in range(SEQ):
        got = proj[LC, pl.ds(s * RES, RES // 4, stride=4), :]
        for p in range(1, 4):
            piece = proj[LC, pl.ds(s * RES + p, RES // 4, stride=4), :]
            got = jnp.where(lane == p, piece, got)
        got = got + b_r
        for c in range(NCOL):
            pay_f[pl.ds(c * RPAY + s * RG, RG), :] = got[c * RG : c * RG + RG]
    rpay[...] = pay_f[: NCOL * RPAY, :].astype(BF).reshape(NCOL, RPAY, 128)
    pl.semaphore_wait(barrier, len(greet))
    s1_r = []
    for n, c in enumerate(r_peers):
        n += len(l_peers)
        s1_r.append(
            pltpu.make_async_remote_copy(
                src_ref=rpay.at[c], dst_ref=rrecv.at[col],
                send_sem=s1_send.at[n], recv_sem=s1_recv.at[n],
                device_id=(row, c), device_id_type=MESH,
            )
        )
        s1_r[-1].start()
    rrecv[col] = rpay[col]

    lane = lax.broadcasted_iota(jnp.int32, (RES // 16, 128), 1) % 16
    for s in range(SEQ):
        for c4 in range(LC):
            got = proj[c4, pl.ds(s * RES, RES // 16, stride=16), :]
            for p in range(1, 16):
                piece = proj[c4, pl.ds(s * RES + p, RES // 16, stride=16), :]
                got = jnp.where(lane == p, piece, got)
            got = got + b_l[:, c4 * 128 : c4 * 128 + 128]
            for r in range(NROW):
                pay_f[pl.ds(r * LPAY + (s * LC + c4) * LB, LB), :] = got[r * LB : r * LB + LB]
    lpay[...] = pay_f[: NROW * LPAY, :].astype(BF).reshape(NROW, LPAY, 128)
    s1_l = []
    for n, (_, r, c) in enumerate(l_peers):
        s1_l.append(
            pltpu.make_async_remote_copy(
                src_ref=lpay.at[r], dst_ref=lrecv.at[at["yl"], row],
                send_sem=s1_send.at[n], recv_sem=s1_recv.at[n],
                device_id=(r, c), device_id_type=MESH,
            )
        )
        s1_l[-1].start()
    lrecv[at["yl"], row] = lpay[row]

    for load in loads[6:]:
        load.wait()
    bd[...] = jnp.zeros_like(bd)

    def spread(p, carry):
        for half in range(2):
            for place in range(2):
                c = 2 * p + (place ^ half)
                rows = wf_v[pl.ds(pl.multiple_of(c * HID, HID), HID), :]
                for q in range(2):
                    at_row = pl.multiple_of(p * 128 + place * 64 + q * HID, HID)
                    bd[half, pl.ds(at_row, HID), q * 128 : q * 128 + 128] = rows
        return carry

    lax.fori_loop(0, HID // 2, spread, 0, unroll=4)

    k, yl, z = at["k"], at["yl"], at["z"]
    sends_l, sends_r, sends_k = {}, {}, {}

    def copy_out(ref, sends, sems, key, step):
        n = len(sends)
        copy = pltpu.make_async_remote_copy(
            src_ref=ref, dst_ref=ref, send_sem=sems[0].at[n], recv_sem=sems[1].at[n],
            device_id=spot(at, **step), device_id_type=MESH,
        )
        copy.start()
        sends[key] = copy

    def tiles(part, away):
        lo, hi = PARTS[part]
        return left.at[pl.ds(lo, hi - lo), k, pl.ds(lax.rem(z + away, 4) * 2, 2)]

    def out_l(key, ref, **step):
        copy_out(ref, sends_l, (l_send, l_recv), key, step)

    def out_r(key, ref, **step):
        copy_out(ref, sends_r, (r_send, r_recv), key, step)

    def out_k(key, ref):
        copy_out(ref, sends_k, (k_send, k_recv), key, dict(k=1))

    def ring_l(part):
        for step in (2, 1, 3):
            out_l((part, step), tiles(part, 0), z=step)
        out_k((part, 0), tiles(part, 0))

    def sent_l(part):
        for step in (2, 1, 3):
            sends_l.get((part, step)).wait_send()

    def arrived_l(part):
        for step in (2, 1, 3):
            sends_l[part, step].wait_recv()
            out_k((part, step), tiles(part, 4 - step))

    def right_of(y, x):
        return right.at[lax.rem(at["yh"] + y, 2) * 4 + lax.rem(at["x"] + x, 4)]

    def near_r(y):
        for step in (1, 3):
            out_r((y, step), right_of(y, 0), x=step)

    for copy in s1_r:
        copy.wait_recv()
    pay_f[: NCOL * RPAY, :] = rrecv[...].reshape(NCOL * RPAY, 128).astype(F32)
    for g in range(RG):
        parts = [pay_f[pl.ds(s * RG + g, NCOL, stride=RPAY), :] for s in range(SEQ)]
        right[row, g] = jnp.concatenate(parts, axis=0).astype(BF)
    out_r("y", right_of(0, 0), yh=1)
    out_r((0, 2), right_of(0, 0), x=2)
    near_r(0)

    for copy in s1_l:
        copy.wait_recv()
    for y in range(2):
        pay_f[: NROW * LPAY, :] = lrecv[y].reshape(NROW * LPAY, 128).astype(F32)
        for b in range(LB):
            for c4 in range(LC):
                parts = [
                    pay_f[pl.ds((s * LC + c4) * LB + b, NROW, stride=LPAY), :] for s in range(SEQ)
                ]
                left[b, k, z * 2 + y, c4] = jnp.concatenate(parts, axis=0).astype(BF)
    ring_l(0)

    sends_r["y"].wait_recv()
    near_r(1)
    sent_l(0)
    ring_l(1)
    sends_r[0, 2].wait_recv()
    out_r((1, 2), right_of(0, 2), yh=1)
    arrived_l(0)
    sent_l(1)
    ring_l(2)
    for key in ((0, 1), (0, 3), (1, 1), (1, 3), (1, 2)):
        sends_r[key].wait_recv()

    def from_core(part):
        for key in range(4):
            sends_k[part, key].wait_recv()

    from_core(0)

    new = lax.broadcasted_iota(jnp.int32, (TOTAL, TOTAL), 0)
    old = lax.broadcasted_iota(jnp.int32, (TOTAL, TOTAL), 1)
    from_col = new // 16 % 2 * 8 + new // 32 % 4 * 2 + new // 128
    perm = (new % 8 * 32 + new // 8 % 2 * 16 + from_col == old).astype(F32).astype(BF)
    for g in range(RG):
        block = jnp.dot(
            perm, right[:, g].reshape(TOTAL, 128), preferred_element_type=F32
        ).astype(BF)
        at_lane = g * 128
        rp[0, :, at_lane : at_lane + 128] = block
        rp[1, :, at_lane : at_lane + 64] = block[:, 64:]
        rp[1, :, at_lane + 64 : at_lane + 128] = block[:, :64]

    low = lax.broadcasted_iota(jnp.int32, (256, 256), 1) % 128 < 64

    def outer(b):
        for c4 in range(LC):
            lt[b * 512 + c4 * 128 : b * 512 + c4 * 128 + 128, :] = jnp.transpose(
                left[b, :, :, c4].reshape(TOTAL, 128)
            )
        for n in range(RG // 2):
            even, odd = (
                jnp.dot(
                    lt[b * 512 + h * 256 : b * 512 + h * 256 + 256, :],
                    rp[h, :, n * 256 : n * 256 + 256],
                    preferred_element_type=F32,
                ).astype(BF)
                for h in range(2)
            )
            for half, x in enumerate((jnp.where(low, even, odd), jnp.where(low, odd, even))):
                for p in range(HID // 2):
                    for g in range(2):
                        at_row = (b * RG + 2 * n + g) * 16
                        xk[half, at_row : at_row + 16, p * 128 : p * 128 + 128] = x[
                            p * 16 : p * 16 + 16, g * 128 : g * 128 + 128
                        ]

    def project(part):
        lo, hi = PARTS[part]
        for half in range(2):
            r = jnp.dot(
                xk[half, lo * 16 * RG : hi * 16 * RG, :], bd[half], preferred_element_type=F32
            )
            for b in range(hi - lo):
                for g in range(RG):
                    for q in range(2):
                        at_row = (lo + b) * 16 * COLS + g * 4 + half * 2 + q
                        from_row = (b * RG + g) * 16
                        acc[pl.ds(at_row, 16, stride=COLS), :] = r[
                            from_row : from_row + 16, q * 128 : q * 128 + 128
                        ]
        rows = slice(lo * 16 * COLS, hi * 16 * COLS)
        update = acc[rows, :] * (1.0 / TOTAL) + bf_ref[...]
        out_ref[rows, :] = (pair_v[rows, :].astype(F32) + update).astype(BF)

    outer(0)
    arrived_l(1)
    outer(1)
    arrived_l(2)
    project(0)
    from_core(1)
    for b in range(*PARTS[1]):
        outer(b)
    project(1)
    from_core(2)
    for b in range(*PARTS[2]):
        outer(b)
    project(2)

    sent_l(2)
    for sends in (sends_r, sends_k):
        for copy in sends.values():
            copy.wait_send()
    for copy in s1_l + s1_r:
        copy.wait_send()


def body(x, scale, w1, b1, w2, b2, wf, bf, pair):
    vmem = pl.BlockSpec(memory_space=pltpu.VMEM)
    hbm = pl.BlockSpec(memory_space=pltpu.HBM)
    dma = pltpu.SemaphoreType.DMA
    n1 = 2 * NROW - 1 + NCOL - 1
    out = pl.pallas_call(
        kernel,
        out_shape=pltpu.VMEM((ROWS * COLS, CP), BF),
        in_specs=[hbm] * 9,
        out_specs=vmem,
        scratch_shapes=[
            pltpu.VMEM((SEQ * RES, FEAT), BF),
            pltpu.VMEM((1, FEAT), F32),
            pltpu.VMEM((HID, FEAT), BF),
            pltpu.VMEM((1, HID), F32),
            pltpu.VMEM((HID, FEAT), BF),
            pltpu.VMEM((1, HID), F32),
            pltpu.VMEM((HID * HID, CP), BF),
            pltpu.VMEM((1, CP), F32),
            pltpu.VMEM((ROWS * COLS, CP), BF),
            pltpu.VMEM((ROWS * COLS, CP), F32),
            pltpu.VMEM((5, SEQ * RES, 128), F32),
            pltpu.VMEM((NCOL * RPAY, 128), F32),
            pltpu.VMEM((NROW, LPAY, 128), BF),
            pltpu.VMEM((NCOL, RPAY, 128), BF),
            pltpu.VMEM((2, NROW, LPAY, 128), BF),
            pltpu.VMEM((NCOL, RPAY, 128), BF),
            pltpu.VMEM((LB, 2, 8, LC, SEQ * NROW, 128), BF),
            pltpu.VMEM((NROW, RG, SEQ * NCOL, 128), BF),
            pltpu.VMEM((ROWS * HID, TOTAL), BF),
            pltpu.VMEM((2, TOTAL, COLS * HID), BF),
            pltpu.VMEM((2, RG * ROWS, HID * 64), BF),
            pltpu.VMEM((2, HID * 64, 2 * CP), BF),
            dma((9,)), dma((n1,)), dma((n1,)),
            dma((9,)), dma((9,)), dma((7,)), dma((7,)), dma((12,)), dma((12,)),
        ],
        compiler_params=pltpu.CompilerParams(
            collective_id=0, has_side_effects=True, vmem_limit_bytes=56 * 2**20
        ),
    )(
        x.reshape(SEQ * RES, FEAT), scale.reshape(1, FEAT), w1.T, b1.reshape(1, HID),
        w2.T, b2.reshape(1, HID), wf, bf.reshape(1, CP),
        pair.reshape(ROWS * COLS, CP),
    )
    return out.reshape(ROWS, COLS, CP)


def solution(mesh):
    return jax.shard_map(
        body,
        mesh=mesh,
        in_specs=(P(("row", "col"), None, None), P(), P(), P(), P(), P(), P(), P(), P("row", "col", None)),
        out_specs=P("row", "col", None),
        check_vma=False,
    )
```

```python
import jax
import jax.numpy as jnp
from jax import lax
from jax.experimental import pallas as pl
from jax.experimental.pallas import tpu as pltpu
from jax.sharding import PartitionSpec as P

BF = jnp.bfloat16
F32 = jnp.float32
MESH = pl.DeviceIdType.MESH

SEQ = 2
RES = 640
FEAT = 256
HID = 32
CP = 128
NROW, NCOL = 8, 16
TOTAL = SEQ * NROW * NCOL
ROWS = RES // NROW
COLS = RES // NCOL
LB, LC = ROWS // 16, HID // 8
LT = LB * LC
RG = COLS // 4
PARTS = ((0, 2), (2, 4), (4, 5))
LPAY, RPAY = 48, 32
CHUNK = 320


def spot(at, **step):
    size = dict(yh=2, x=4, yl=2, z=4, k=2)
    to = {a: lax.rem(at[a] + step[a], size[a]) if a in step else at[a] for a in at}
    return to["yh"] * 4 + to["x"], (to["yl"] * 4 + to["z"]) * 2 + to["k"]


def kernel(
    x_hbm, scale_hbm, w1_hbm, b1_hbm, w2_hbm, b2_hbm, wf_hbm, bf_hbm, pair_hbm, out_ref,
    x_v, scale_ref, w1_ref, b1_ref, w2_ref, b2_ref, wf_v, bf_ref, pair_v, acc, proj, pay_f, lpay, rpay, lrecv, rrecv, left, right,
    lt, rp, xk, bd,
    load_sem, s1_send, s1_recv, l_send, l_recv, r_send, r_recv, k_send, k_recv,
):
    row, col = lax.axis_index("row"), lax.axis_index("col")
    at = dict(yh=row // 4, x=row % 4, yl=col // 8, z=(col // 2) % 4, k=col % 2)

    loads = [
        pltpu.make_async_copy(source, held, load_sem.at[n])
        for n, (source, held) in enumerate((
            (w1_hbm, w1_ref), (w2_hbm, w2_ref), (b1_hbm, b1_ref), (b2_hbm, b2_ref),
            (scale_hbm, scale_ref), (x_hbm, x_v), (wf_hbm, wf_v), (bf_hbm, bf_ref),
            (pair_hbm, pair_v),
        ))
    ]
    for load in loads:
        load.start()

    other = lax.rem(col + NCOL // 2, NCOL)
    l_peers = [(k, lax.rem(row + k, NROW), c) for c in (col, other) for k in range(NROW)][1:]
    r_peers = [lax.rem(col + k, NCOL) for k in range(1, NCOL)]
    greet = [(r, c) for k, r, c in l_peers if k > 0] + [(row, c) for c in r_peers]
    barrier = pltpu.get_barrier_semaphore()
    for peer in greet:
        pl.semaphore_signal(barrier, inc=1, device_id=peer, device_id_type=MESH)

    for load in loads[:5]:
        load.wait()
    wide = lax.broadcasted_iota(jnp.int32, (512, HID), 0) // 16
    wide = wide % 16 * 2 + wide // 16
    sel_l = (wide == lax.broadcasted_iota(jnp.int32, (512, HID), 1)).astype(F32)
    wide = lax.broadcasted_iota(jnp.int32, (128, HID), 0) % 32
    sel_r = (wide == lax.broadcasted_iota(jnp.int32, (128, HID), 1)).astype(F32)
    w_l = jnp.dot(sel_l.astype(BF), w1_ref[...], preferred_element_type=F32).astype(BF)
    w_r = jnp.dot(sel_r.astype(BF), w2_ref[...], preferred_element_type=F32).astype(BF)
    across = (((1,), (1,)), ((), ()))
    exact = dict(precision=lax.Precision.HIGHEST, preferred_element_type=F32)
    b_l = lax.dot_general(b1_ref[...], sel_l, across, **exact)
    b_r = lax.dot_general(b2_ref[...], sel_r, across, **exact)
    scale = scale_ref[...]

    loads[5].wait()

    def norm(i):
        rows = pl.ds(i * CHUNK, CHUNK)
        x = x_v[rows, :].astype(F32)
        mean = jnp.sum(x, axis=1, keepdims=True) * (1.0 / FEAT)
        dev = x - mean
        var = jnp.sum(dev * dev, axis=1, keepdims=True) * (1.0 / FEAT)
        normed = (dev * lax.rsqrt(var + 1e-5) * scale).astype(BF)
        p_l = lax.dot_general(normed, w_l, across, preferred_element_type=F32)
        for c4 in range(LC):
            proj[c4, rows, :] = p_l[:, c4 * 128 : c4 * 128 + 128]
        proj[LC, rows, :] = lax.dot_general(
            normed, w_r, across, preferred_element_type=F32
        )

    for i in range(SEQ * RES // CHUNK):
        norm(i)

    lane = lax.broadcasted_iota(jnp.int32, (RES // 4, 128), 1) // 32
    for s in range(SEQ):
        got = proj[LC, pl.ds(s * RES, RES // 4, stride=4), :]
        for p in range(1, 4):
            piece = proj[LC, pl.ds(s * RES + p, RES // 4, stride=4), :]
            got = jnp.where(lane == p, piece, got)
        got = got + b_r
        for c in range(NCOL):
            pay_f[pl.ds(c * RPAY + s * RG, RG), :] = got[c * RG : c * RG + RG]
    rpay[...] = pay_f[: NCOL * RPAY, :].astype(BF).reshape(NCOL, RPAY, 128)
    pl.semaphore_wait(barrier, len(greet))
    s1_r = []
    for n, c in enumerate(r_peers):
        n += len(l_peers)
        s1_r.append(
            pltpu.make_async_remote_copy(
                src_ref=rpay.at[c], dst_ref=rrecv.at[col],
                send_sem=s1_send.at[n], recv_sem=s1_recv.at[n],
                device_id=(row, c), device_id_type=MESH,
            )
        )
        s1_r[-1].start()
    rrecv[col] = rpay[col]

    lane = lax.broadcasted_iota(jnp.int32, (RES // 16, 128), 1) % 16
    for s in range(SEQ):
        for c4 in range(LC):
            got = proj[c4, pl.ds(s * RES, RES // 16, stride=16), :]
            for p in range(1, 16):
                piece = proj[c4, pl.ds(s * RES + p, RES // 16, stride=16), :]
                got = jnp.where(lane == p, piece, got)
            got = got + b_l[:, c4 * 128 : c4 * 128 + 128]
            for r in range(NROW):
                pay_f[pl.ds(r * LPAY + (s * LC + c4) * LB, LB), :] = got[r * LB : r * LB + LB]
    lpay[...] = pay_f[: NROW * LPAY, :].astype(BF).reshape(NROW, LPAY, 128)
    s1_l = []
    for n, (_, r, c) in enumerate(l_peers):
        s1_l.append(
            pltpu.make_async_remote_copy(
                src_ref=lpay.at[r], dst_ref=lrecv.at[at["yl"], row],
                send_sem=s1_send.at[n], recv_sem=s1_recv.at[n],
                device_id=(r, c), device_id_type=MESH,
            )
        )
        s1_l[-1].start()
    lrecv[at["yl"], row] = lpay[row]

    for load in loads[6:]:
        load.wait()
    bd[...] = jnp.zeros_like(bd)

    def spread(p, carry):
        for half in range(2):
            for place in range(2):
                c = 2 * p + (place ^ half)
                rows = wf_v[pl.ds(pl.multiple_of(c * HID, HID), HID), :]
                for q in range(2):
                    at_row = pl.multiple_of(p * 128 + place * 64 + q * HID, HID)
                    bd[half, pl.ds(at_row, HID), q * 128 : q * 128 + 128] = rows
        return carry

    lax.fori_loop(0, HID // 2, spread, 0, unroll=4)

    k, yl, z = at["k"], at["yl"], at["z"]
    sends_l, sends_r, sends_k = {}, {}, {}

    def copy_out(ref, sends, sems, key, step):
        n = len(sends)
        copy = pltpu.make_async_remote_copy(
            src_ref=ref, dst_ref=ref, send_sem=sems[0].at[n], recv_sem=sems[1].at[n],
            device_id=spot(at, **step), device_id_type=MESH,
        )
        copy.start()
        sends[key] = copy

    def tiles(part, away):
        lo, hi = PARTS[part]
        return left.at[pl.ds(lo, hi - lo), k, pl.ds(lax.rem(z + away, 4) * 2, 2)]

    def out_l(key, ref, **step):
        copy_out(ref, sends_l, (l_send, l_recv), key, step)

    def out_r(key, ref, **step):
        copy_out(ref, sends_r, (r_send, r_recv), key, step)

    def out_k(key, ref):
        copy_out(ref, sends_k, (k_send, k_recv), key, dict(k=1))

    def ring_l(part):
        for step in (2, 1, 3):
            out_l((part, step), tiles(part, 0), z=step)
        out_k((part, 0), tiles(part, 0))

    def sent_l(part):
        for step in (2, 1, 3):
            sends_l.get((part, step)).wait_send()

    def arrived_l(part):
        for step in (2, 1, 3):
            sends_l[part, step].wait_recv()
            out_k((part, step), tiles(part, 4 - step))

    def right_of(y, x):
        return right.at[lax.rem(at["yh"] + y, 2) * 4 + lax.rem(at["x"] + x, 4)]

    def near_r(y):
        for step in (1, 3):
            out_r((y, step), right_of(y, 0), x=step)

    for copy in s1_r:
        copy.wait_recv()
    pay_f[: NCOL * RPAY, :] = rrecv[...].reshape(NCOL * RPAY, 128).astype(F32)
    for g in range(RG):
        parts = [pay_f[pl.ds(s * RG + g, NCOL, stride=RPAY), :] for s in range(SEQ)]
        right[row, g] = jnp.concatenate(parts, axis=0).astype(BF)
    out_r("y", right_of(0, 0), yh=1)
    out_r((0, 2), right_of(0, 0), x=2)
    near_r(0)

    for copy in s1_l:
        copy.wait_recv()
    for y in range(2):
        pay_f[: NROW * LPAY, :] = lrecv[y].reshape(NROW * LPAY, 128).astype(F32)
        for b in range(LB):
            for c4 in range(LC):
                parts = [
                    pay_f[pl.ds((s * LC + c4) * LB + b, NROW, stride=LPAY), :] for s in range(SEQ)
                ]
                left[b, k, z * 2 + y, c4] = jnp.concatenate(parts, axis=0).astype(BF)
    ring_l(0)

    sends_r["y"].wait_recv()
    near_r(1)
    sent_l(0)
    ring_l(1)
    sends_r[0, 2].wait_recv()
    out_r((1, 2), right_of(0, 2), yh=1)
    arrived_l(0)
    sent_l(1)
    ring_l(2)
    for key in ((0, 1), (0, 3), (1, 1), (1, 3), (1, 2)):
        sends_r[key].wait_recv()

    def from_core(part):
        for key in range(4):
            sends_k[part, key].wait_recv()

    from_core(0)

    new = lax.broadcasted_iota(jnp.int32, (TOTAL, TOTAL), 0)
    old = lax.broadcasted_iota(jnp.int32, (TOTAL, TOTAL), 1)
    from_col = new // 16 % 2 * 8 + new // 32 % 4 * 2 + new // 128
    perm = (new % 8 * 32 + new // 8 % 2 * 16 + from_col == old).astype(F32).astype(BF)
    for g in range(RG):
        block = jnp.dot(
            perm, right[:, g].reshape(TOTAL, 128), preferred_element_type=F32
        ).astype(BF)
        at_lane = g * 128
        rp[0, :, at_lane : at_lane + 128] = block
        rp[1, :, at_lane : at_lane + 64] = block[:, 64:]
        rp[1, :, at_lane + 64 : at_lane + 128] = block[:, :64]

    low = lax.broadcasted_iota(jnp.int32, (256, 256), 1) % 128 < 64

    def outer(b):
        for c4 in range(LC):
            lt[b * 512 + c4 * 128 : b * 512 + c4 * 128 + 128, :] = jnp.transpose(
                left[b, :, :, c4].reshape(TOTAL, 128)
            )
        for n in range(RG // 2):
            even, odd = (
                jnp.dot(
                    lt[b * 512 + h * 256 : b * 512 + h * 256 + 256, :],
                    rp[h, :, n * 256 : n * 256 + 256],
                    preferred_element_type=F32,
                ).astype(BF)
                for h in range(2)
            )
            for half, x in enumerate((jnp.where(low, even, odd), jnp.where(low, odd, even))):
                for p in range(HID // 2):
                    for g in range(2):
                        at_row = (b * RG + 2 * n + g) * 16
                        xk[half, at_row : at_row + 16, p * 128 : p * 128 + 128] = x[
                            p * 16 : p * 16 + 16, g * 128 : g * 128 + 128
                        ]

    def project(part):
        lo, hi = PARTS[part]
        for half in range(2):
            r = jnp.dot(
                xk[half, lo * 16 * RG : hi * 16 * RG, :], bd[half], preferred_element_type=F32
            )
            for b in range(hi - lo):
                for g in range(RG):
                    for q in range(2):
                        at_row = (lo + b) * 16 * COLS + g * 4 + half * 2 + q
                        from_row = (b * RG + g) * 16
                        acc[pl.ds(at_row, 16, stride=COLS), :] = r[
                            from_row : from_row + 16, q * 128 : q * 128 + 128
                        ]
        rows = slice(lo * 16 * COLS, hi * 16 * COLS)
        update = acc[rows, :] * (1.0 / TOTAL) + bf_ref[...]
        out_ref[rows, :] = (pair_v[rows, :].astype(F32) + update).astype(BF)

    outer(0)
    arrived_l(1)
    outer(1)
    project(0)
    arrived_l(2)
    from_core(1)
    for b in range(*PARTS[1]):
        outer(b)
    project(1)
    from_core(2)
    for b in range(*PARTS[2]):
        outer(b)
    project(2)

    sent_l(2)
    for sends in (sends_r, sends_k):
        for copy in sends.values():
            copy.wait_send()
    for copy in s1_l + s1_r:
        copy.wait_send()


def body(x, scale, w1, b1, w2, b2, wf, bf, pair):
    vmem = pl.BlockSpec(memory_space=pltpu.VMEM)
    hbm = pl.BlockSpec(memory_space=pltpu.HBM)
    dma = pltpu.SemaphoreType.DMA
    n1 = 2 * NROW - 1 + NCOL - 1
    out = pl.pallas_call(
        kernel,
        out_shape=pltpu.VMEM((ROWS * COLS, CP), BF),
        in_specs=[hbm] * 9,
        out_specs=vmem,
        scratch_shapes=[
            pltpu.VMEM((SEQ * RES, FEAT), BF),
            pltpu.VMEM((1, FEAT), F32),
            pltpu.VMEM((HID, FEAT), BF),
            pltpu.VMEM((1, HID), F32),
            pltpu.VMEM((HID, FEAT), BF),
            pltpu.VMEM((1, HID), F32),
            pltpu.VMEM((HID * HID, CP), BF),
            pltpu.VMEM((1, CP), F32),
            pltpu.VMEM((ROWS * COLS, CP), BF),
            pltpu.VMEM((ROWS * COLS, CP), F32),
            pltpu.VMEM((5, SEQ * RES, 128), F32),
            pltpu.VMEM((NCOL * RPAY, 128), F32),
            pltpu.VMEM((NROW, LPAY, 128), BF),
            pltpu.VMEM((NCOL, RPAY, 128), BF),
            pltpu.VMEM((2, NROW, LPAY, 128), BF),
            pltpu.VMEM((NCOL, RPAY, 128), BF),
            pltpu.VMEM((LB, 2, 8, LC, SEQ * NROW, 128), BF),
            pltpu.VMEM((NROW, RG, SEQ * NCOL, 128), BF),
            pltpu.VMEM((ROWS * HID, TOTAL), BF),
            pltpu.VMEM((2, TOTAL, COLS * HID), BF),
            pltpu.VMEM((2, RG * ROWS, HID * 64), BF),
            pltpu.VMEM((2, HID * 64, 2 * CP), BF),
            dma((9,)), dma((n1,)), dma((n1,)),
            dma((9,)), dma((9,)), dma((7,)), dma((7,)), dma((12,)), dma((12,)),
        ],
        compiler_params=pltpu.CompilerParams(
            collective_id=0, has_side_effects=True, vmem_limit_bytes=56 * 2**20
        ),
    )(
        x.reshape(SEQ * RES, FEAT), scale.reshape(1, FEAT), w1.T, b1.reshape(1, HID),
        w2.T, b2.reshape(1, HID), wf, bf.reshape(1, CP),
        pair.reshape(ROWS * COLS, CP),
    )
    return out.reshape(ROWS, COLS, CP)


def solution(mesh):
    return jax.shard_map(
        body,
        mesh=mesh,
        in_specs=(P(("row", "col"), None, None), P(), P(), P(), P(), P(), P(), P(), P("row", "col", None)),
        out_specs=P("row", "col", None),
        check_vma=False,
    )
```
